32 devices in a mesh: dp: 8 (over y, x, core), ctx: 4 (over z).
Axes of the slice: x: 2, y: 2, z: 4, core: 2. Of those that a mesh axis runs over, the one named last changes fastest.
Arguments:
- cotangent: bfloat16 [8, 2048, 8192], P('dp', 'ctx'), may hold values from -6 to 6
- out_weight: bfloat16 [256, 8192], P(None, 'ctx'), may hold values from -0.0625 to 0.0625
- head_input: bfloat16 [8, 2048, 256], P('dp', 'ctx'), may hold values from -6 to 6
- injector: bfloat16 [8, 2048, 128], P('dp', 'ctx'), may hold values from -0.59765625 to 0.59765625
- readout: bfloat16 [8, 2048, 128], P('dp', 'ctx'), may hold values from -0.59765625 to 0.59765625
- decay_code: int32 [8, 2048, 2], P('dp', 'ctx'), may hold values from 1 to 20480
- decay_rate: float32 [2], replicated, may hold values from 9.765625e-06 to 0.012207031
- start_state: float32 [8, 4, 2, 128, 128], P('dp', 'ctx'), may hold values from -6 to 6
Outputs:
- gradient_input: bfloat16 [8, 2048, 256], P('dp', 'ctx')
- gradient_injector: float32 [8, 2048, 128], P('dp', 'ctx')
- gradient_readout: float32 [8, 2048, 128], P('dp', 'ctx')
- gradient_weight: float32 [256, 8192], P('ctx', 'dp')
- gradient_rate: float32 [2], replicated
The draws below stay inside these ranges and needn't reach their ends.
All inputs are finite; a program needn't handle non-finite values.
Results may differ from the reference program's by a relative error of at most 0.0049.
Values may be sent and summed in bfloat16 or wider, within the bound.
A program may use at most 128 MiB of HBM per device.

```python
import math
import jax
import jax.numpy as jnp
from jax import lax

D = 8192
P_SIZE = 128
N = 128
H = 2
S_DEV = 512
SEQUENCE_COUNT = 8
SEQUENCE_LENGTH = 2048
HP = 256
N_CTX = 4


def draw_decay_code(key, part):
    key_base = jax.random.fold_in(key, 11)
    key_unit = jax.random.fold_in(key, 12)
    spike_key = jax.random.fold_in(key, 13)
    base_level = jax.random.randint(key_base, (SEQUENCE_COUNT, SEQUENCE_LENGTH // S_DEV, 1, H), 2, 9)
    base_level = jnp.broadcast_to(base_level, (SEQUENCE_COUNT, SEQUENCE_LENGTH // S_DEV, S_DEV, H)).reshape(SEQUENCE_COUNT, SEQUENCE_LENGTH, H)
    uniform_bits = jax.random.randint(key_unit, (SEQUENCE_COUNT, SEQUENCE_LENGTH, H), 0, 1 << 20)
    encoded_values = 1 + uniform_bits % (2 * base_level)
    location_list = jax.random.randint(spike_key, (SEQUENCE_COUNT, 3, 1), 0, SEQUENCE_LENGTH)
    token_position = lax.broadcasted_iota(jnp.int32, (SEQUENCE_COUNT, 3, SEQUENCE_LENGTH), 2)
    spike_mask = jnp.any(token_position == location_list, axis=1)
    return jnp.where(spike_mask[:, :, None], 10 * SEQUENCE_LENGTH, encoded_values).astype(jnp.int32)


def draw_decay_rate(key, part):
    low_end, high_end = (0.02, 25.0)
    spread = jax.random.uniform(key, (H,), jnp.float32, math.log(low_end), math.log(high_end))
    return (jnp.exp(spread) / SEQUENCE_LENGTH).astype(jnp.float32)


def raised(entries, key, source, target, blocks, factor):
    def block_of(dim):
        return (jnp.arange(entries.shape[dim]) // (entries.shape[dim] // blocks)).reshape((-1,) + (1,) * (entries.ndim - 1 - dim))

    first = jax.random.permutation(key, blocks)[block_of(target)]
    other_side = (block_of(target) + blocks // 2) % blocks
    return jnp.where((block_of(source) == first) | (block_of(source) == other_side), factor * entries, entries)


def level_of(stream_key, dims, split, low, top_value):
    def one(axis_at, blocks):
        steps = jax.random.uniform(jax.random.fold_in(jax.random.fold_in(stream_key, 6), axis_at), (blocks,), jnp.float32, low / len(split), top_value / len(split))
        return jnp.repeat(jnp.exp(steps), dims[axis_at] // blocks).reshape((-1,) + (1,) * (len(dims) - axis_at - 1))

    level = one(*split[0])
    for cut in split[1:]:
        level = level * one(*cut)
    return level


def noise(own_key, shape, width, reach, cuts=(), held_as=jnp.bfloat16):
    drawn = width * jax.random.normal(own_key, shape, jnp.float32)
    if cuts:
        drawn = drawn * level_of(own_key, shape, cuts, -0.22, 0.18)
    return jnp.clip(drawn, -reach, reach).astype(held_as)


def bell_draw_with(own_key, dims, scale, most, cuts, heavy, kind=jnp.bfloat16):
    result = scale * jax.random.normal(own_key, dims, jnp.float32)
    if cuts:
        result = result * level_of(own_key, dims, cuts, -0.22, 0.18)
    return jnp.clip(raised(result, jax.random.fold_in(own_key, 3), *heavy), -most, most).astype(kind)


def setup_inputs(seed: int = 0) -> dict:
    key_list = jax.random.split(jax.random.key(seed), 9)
    cotangent = bell_draw_with(key_list[0], (SEQUENCE_COUNT, SEQUENCE_LENGTH, D), 1.0, 6.0, ((0, 8), (1, 4)), (0, 2, 8, 2.0))
    out_weight = noise(key_list[1], (HP, D), D ** -0.5, 0.0625, ((1, 4),))
    head_input = noise(key_list[2], (SEQUENCE_COUNT, SEQUENCE_LENGTH, HP), 1.0, 6.0, ((0, 8), (1, 4)))
    injector = noise(key_list[3], (SEQUENCE_COUNT, SEQUENCE_LENGTH, N), 0.1, 0.59765625, ((0, 8), (1, 4)))
    readout = noise(key_list[4], (SEQUENCE_COUNT, SEQUENCE_LENGTH, N), 0.1, 0.59765625, ((0, 8), (1, 4)))
    decay_code = draw_decay_code(jax.random.fold_in(key_list[8], 71), 0)
    decay_rate = draw_decay_rate(jax.random.fold_in(key_list[8], 71), 0)
    start_state = noise(key_list[7], (SEQUENCE_COUNT, N_CTX, H, P_SIZE, N), 1.0, 6.0, ((0, 8), (1, 4)), jnp.float32)
    return dict(cotangent=cotangent, out_weight=out_weight, head_input=head_input, injector=injector, readout=readout, decay_code=decay_code, decay_rate=decay_rate, start_state=start_state)


precise = lax.Precision.HIGHEST


def decay_table(log_decay):
    cumulative = jnp.cumsum(log_decay, axis=0)
    length = log_decay.shape[0]
    row_index = lax.broadcasted_iota(jnp.int32, (length, length), 0)
    col_index = lax.broadcasted_iota(jnp.int32, (length, length), 1)
    causal = (row_index >= col_index)[None]
    spread = cumulative.T[:, :, None] - cumulative.T[:, None, :]
    weights = jnp.where(causal, jnp.exp(jnp.where(causal, spread, 0.0)), 0.0)
    return cumulative, weights


def forward_shard(head_input, injector, readout, log_decay, start_state):
    length, heads_count = log_decay.shape
    cumulative, weights = decay_table(log_decay)
    intersection = jnp.dot(readout, injector.T, preferred_element_type=jnp.float32)
    mixing = intersection[None] * weights
    inputs_heads = head_input.reshape(length, heads_count, -1).astype(jnp.float32)
    within = jnp.einsum("hts,shp->thp", mixing, inputs_heads, precision=precise)
    carried = jnp.einsum("tn,hpn->thp", readout.astype(jnp.float32), start_state, precision=precise)
    outputs = within + jnp.exp(cumulative)[:, :, None] * carried
    return outputs.reshape(length, -1).astype(jnp.bfloat16)


def chain_piece(readout, output_grad, log_decay):
    length, heads_count = log_decay.shape
    cumulative = jnp.cumsum(log_decay, axis=0)
    grad_heads = output_grad.reshape(length, heads_count, -1).astype(jnp.float32)
    scaled = jnp.exp(cumulative)[:, :, None] * readout.astype(jnp.float32)[:, None, :]
    adjoint = jnp.einsum("thp,thn->hpn", grad_heads, scaled, precision=precise)
    return jnp.exp(cumulative[-1]), adjoint


def backward_shard(head_input, injector, readout, output_grad, log_decay, start_state, incoming):
    length, heads_count = log_decay.shape
    cumulative, weights = decay_table(log_decay)
    inputs_heads = head_input.reshape(length, heads_count, -1).astype(jnp.float32)
    grad_heads = output_grad.reshape(length, heads_count, -1).astype(jnp.float32)
    inject_float = injector.astype(jnp.float32)
    read_float = readout.astype(jnp.float32)
    intersection = jnp.dot(readout, injector.T, preferred_element_type=jnp.float32)
    mixing = intersection[None] * weights
    to_end = jnp.exp(cumulative[-1][None, :] - cumulative)
    from_start = jnp.exp(cumulative)
    entering = jnp.einsum("sn,hpn->shp", inject_float, incoming, precision=precise)
    grad_input = jnp.einsum("hts,thp->shp", mixing, grad_heads, precision=precise) + to_end[:, :, None] * entering
    pairing = jnp.einsum("thp,shp->hts", grad_heads, inputs_heads, precision=precise) * weights
    through_start = jnp.einsum("thp,hpn->thn", grad_heads, start_state, precision=precise)
    grad_read = jnp.einsum("hts,sn->tn", pairing, inject_float, precision=precise)
    grad_read = grad_read + jnp.einsum("th,thn->tn", from_start, through_start, precision=precise)
    input_state = jnp.einsum("shp,hpn->shn", inputs_heads, incoming, precision=precise)
    grad_inject = jnp.einsum("hts,tn->sn", pairing, read_float, precision=precise)
    grad_inject = grad_inject + jnp.einsum("sh,shn->sn", to_end, input_state, precision=precise)
    products = intersection[None] * pairing
    carried = jnp.einsum("tn,hpn->thp", read_float, start_state, precision=precise) * from_start[:, :, None]
    reaching = to_end * jnp.einsum("shn,sn->sh", input_state, inject_float, precision=precise)
    end_term = from_start[-1] * jnp.einsum("hpn,hpn->h", incoming, start_state, precision=precise) + jnp.sum(reaching, axis=0)
    cumul_grad = jnp.sum(products, axis=2).T - jnp.sum(products, axis=1).T
    cumul_grad = cumul_grad + jnp.sum(grad_heads * carried, axis=2) - reaching
    is_last = lax.broadcasted_iota(jnp.int32, (length, 1), 0) == length - 1
    cumul_grad = cumul_grad + jnp.where(is_last, end_term[None, :], 0.0)
    decay_grad = jnp.flip(jnp.cumsum(jnp.flip(cumul_grad, 0), axis=0), 0)
    rate_terms = jnp.sum(decay_grad * log_decay, axis=0)
    return grad_input.reshape(length, -1).astype(jnp.bfloat16), grad_inject, grad_read, rate_terms


def reference(cotangent, out_weight, head_input, injector, readout, decay_code, decay_rate, start_state):
    pieces_count = SEQUENCE_LENGTH // S_DEV

    def to_pieces(array):
        return array.reshape((pieces_count, S_DEV) + array.shape[1:])

    def per_sequence(totals, sequence):
        weight_total, rate_total = totals
        grad_out, inputs_seq, inject_seq, read_seq, code_seq, states_seq = sequence
        output_grad = jnp.dot(grad_out, out_weight.T, preferred_element_type=jnp.float32).astype(jnp.bfloat16)
        log_decay = -decay_rate[None, :] * code_seq.astype(jnp.float32)
        pieces = (to_pieces(inputs_seq), to_pieces(inject_seq), to_pieces(read_seq), to_pieces(output_grad), to_pieces(log_decay))
        outputs = lax.map(lambda group: forward_shard(group[0], group[1], group[2], group[4], group[5]), pieces + (states_seq,))
        scales, adjoints = lax.map(lambda group: chain_piece(group[2], group[3], group[4]), pieces)

        def backward_step(incoming, element):
            return element[1] + element[0][:, None, None] * incoming, incoming

        _, incomings = lax.scan(backward_step, jnp.zeros_like(adjoints[0]), (scales, adjoints), reverse=True)
        grad_input, grad_inject, grad_read, rate_terms = lax.map(lambda group: backward_shard(*group), pieces + (states_seq, incomings))
        whole_out = outputs.reshape(SEQUENCE_LENGTH, -1)
        weight_total = weight_total + jnp.dot(whole_out.T, grad_out, preferred_element_type=jnp.float32)
        rate_total = rate_total + jnp.sum(rate_terms, axis=0)
        return (weight_total, rate_total), (grad_input.reshape(SEQUENCE_LENGTH, -1), grad_inject.reshape(SEQUENCE_LENGTH, -1), grad_read.reshape(SEQUENCE_LENGTH, -1))

    initial = (jnp.zeros((H * P_SIZE, D), jnp.float32), jnp.zeros((H,), jnp.float32))
    (weight_total, rate_total), (gradient_input, gradient_injector, gradient_readout) = lax.scan(
        per_sequence, initial, (cotangent, head_input, injector, readout, decay_code, start_state))
    return gradient_input, gradient_injector, gradient_readout, weight_total, rate_total / (SEQUENCE_COUNT * SEQUENCE_LENGTH)
```

```python
import functools

import jax
import jax.numpy as jnp
from jax import lax
from jax.experimental import pallas as pl
from jax.experimental.pallas import tpu as pltpu
from jax.sharding import PartitionSpec as P

F32, BF16 = jnp.float32, jnp.bfloat16
MESH = pl.DeviceIdType.MESH


def nn(a, b):
    return lax.dot_general(a, b, (((1,), (0,)), ((), ())), preferred_element_type=F32)


def nt(a, b):
    return lax.dot_general(a, b, (((1,), (1,)), ((), ())), preferred_element_type=F32)


def halves(value):
    high = value.astype(BF16)
    return high, (value - high.astype(F32)).astype(BF16)


def fold(row):
    total = row[:, :128]
    for at in range(128, row.shape[1], 128):
        total = total + row[:, at : at + 128]
    return total


def kernel(
    n, dps,
    rate_ref, cot_hbm, w_ref, x_ref, inj_ref, read_ref, codecol_ref, coderow_ref, start_ref,
    gi_ref, ginj_ref, gread_ref, gw_ref, rate_out,
    cot, wslot, acc, own, part_send, part_recv, plane_send, plane_recv, zsend, zrecv,
    fwd_t, mix_t, wts, wts_t, qts, scal, inc, chain_send, rate_z, rate_dp, rate_mine, rate_mid,
    cot_sem, send_sem, zsem, psem, csem, asem, bsem, dsem, chsem, r1sem, r2sem,
):
    length, heads = x_ref.shape[0], start_ref.shape[0]
    dz = w_ref.shape[1]
    chips = dps // 2
    rows, cols = gw_ref.shape
    dp, c = lax.axis_index("dp"), lax.axis_index("ctx")
    chip, core = lax.div(dp, 2), lax.rem(dp, 2)
    partner = (chip * 2 + 1 - core, c)
    quarter = w_ref.shape[0] // 4
    sent = []
    counter = [0]

    def send(src, dst, recv_sem, device, cond=None):
        index = counter[0]
        counter[0] += 1
        copy = pltpu.make_async_remote_copy(
            src_ref=src, dst_ref=dst, send_sem=send_sem.at[index], recv_sem=recv_sem,
            device_id=device, device_id_type=MESH,
        )
        sent.append((copy, cond))
        if cond is None:
            copy.start()
        else:
            pl.when(cond)(lambda: copy.start())

    def arrived(dst, recv_sem):
        pltpu.make_async_copy(dst, dst, recv_sem).wait()

    loads = []
    for i in range(4):
        r = pl.ds(i * (length // 4), length // 4)
        load = pltpu.make_async_copy(cot_hbm.at[r], cot.at[r], cot_sem.at[i])
        load.start()
        loads.append(load)

    barrier = pltpu.get_barrier_semaphore()
    for i in range(1, dps):
        pl.semaphore_signal(barrier, inc=1, device_id=(lax.rem(dp + i, dps), c), device_id_type=MESH)
    for i in range(1, n):
        pl.semaphore_signal(barrier, inc=1, device_id=(dp, lax.rem(c + i, n)), device_id_type=MESH)
    pl.semaphore_wait(barrier, dps + n - 2)

    def shard_place(shard):
        par = lax.rem(shard, 2)
        bit = lax.rem(chip, 2) * (1 - par) + lax.rem(lax.div(chip, 2), 2) * par
        peer = chip + (1 - 2 * bit) * (1 + par)
        return bit, peer

    def q_rows(k, bit):
        return pl.ds(pl.multiple_of((2 * k + bit) * quarter, quarter), quarter)

    bit, _ = shard_place(c)
    mine = q_rows(core, bit)
    send(w_ref.at[mine], wslot.at[0, 0, mine], zsem.at[0, 0], (dp, lax.rem(c + 1, n)), c + 1 < n)
    send(w_ref.at[mine], wslot.at[1, 0, mine], zsem.at[1, 0], (dp, lax.rem(c + n - 1, n)), c > 0)

    def shard_of(way, step):
        return (c - 1 - step, c - 1 - step >= 0) if way == 0 else (c + 1 + step, c + 1 + step < n)

    def w_z(step):
        for way in range(2):
            shard, valid = shard_of(way, step)
            shard = lax.rem(shard + n, n)
            bit, peer = shard_place(shard)
            here = q_rows(core, bit)
            slot = wslot.at[way, step, here]
            pl.when(valid)(lambda: arrived(slot, zsem.at[way, step]))
            if step + 1 < n - 1:
                if way == 0:
                    send(slot, wslot.at[way, step + 1, here], zsem.at[way, step + 1],
                         (dp, lax.rem(c + 1, n)), valid & (c + 1 < n))
                else:
                    send(slot, wslot.at[way, step + 1, here], zsem.at[way, step + 1],
                         (dp, lax.rem(c + n - 1, n)), valid & (c > 0))
            send(slot, slot, psem.at[way, step], (peer * 2 + core, c), valid)
            send(slot, slot, csem.at[way, step, 0], partner, valid)

    def w_plane(step):
        for way in range(2):
            shard, valid = shard_of(way, step)
            shard = lax.rem(shard + n, n)
            bit, _ = shard_place(shard)
            slot = wslot.at[way, step, q_rows(core, 1 - bit)]
            pl.when(valid)(lambda: arrived(slot, psem.at[way, step]))
            send(slot, slot, csem.at[way, step, 1], partner, valid)

    def w_use(step):
        for way in range(2):
            shard, valid = shard_of(way, step)
            shard = lax.rem(shard + n, n)
            bit, _ = shard_place(shard)

            @pl.when(valid)
            def _():
                for which in range(2):
                    there = bit if which == 0 else 1 - bit
                    arrived(wslot.at[way, step, q_rows(1 - core, there)], csem.at[way, step, which])
                at = pl.ds(pl.multiple_of(shard * dz, dz), dz)
                acc[...] += nt(cot[:, at], wslot[way, step])

    row_at = lax.broadcasted_iota(jnp.int32, (length, length), 0)
    col_at = lax.broadcasted_iota(jnp.int32, (length, length), 1)
    lower = row_at >= col_at
    upper = col_at >= row_at
    col_sum = nn(jnp.where(lower, 1.0, 0.0).astype(BF16), codecol_ref[...])
    row_sum = nn(coderow_ref[...], jnp.where(upper, 1.0, 0.0).astype(BF16))
    inter_t = nt(inj_ref[...], read_ref[...])
    x_t = x_ref[...].astype(F32).T.astype(BF16)
    cum_col, cum_row = [], []
    for h in range(heads):
        ch = slice(h * 128, (h + 1) * 128)
        rate = rate_ref[h]
        cc = -rate * (256.0 * col_sum[:, h : h + 1] + col_sum[:, heads + h : heads + h + 1])
        cr = -rate * (256.0 * row_sum[h : h + 1] + row_sum[heads + h : heads + h + 1])
        cum_col.append(cc)
        cum_row.append(cr)
        w_t = jnp.where(upper, jnp.exp(jnp.where(upper, cr - cc, 0.0)), 0.0)
        wts_t[h] = w_t
        mixed = (inter_t * w_t).astype(BF16)
        mix_t[h] = mixed
        high, low = halves(start_ref[h])
        carried = nt(high, read_ref[...]) + nt(low, read_ref[...])
        fwd_t[ch, :] = (nn(x_t[ch], mixed) + jnp.exp(cr) * carried).astype(BF16)

    for load in loads:
        load.wait()

    def block(chip_at, core_at):
        at = pl.ds(pl.multiple_of((chip_at * 2 + core_at) * cols, cols), cols)
        return nn(fwd_t[...], cot[:, at])

    order = list(range(1, chips)) + [0]
    for i in order:
        target = lax.rem(chip + i, chips)
        part_send[i] = block(target, 1 - core).astype(BF16)
        send(part_send.at[i], part_recv.at[i], asem.at[i], partner)
    w_z(0)
    for i in order:
        target = lax.rem(chip + i, chips)
        own[i] = block(target, core)
        arrived(part_recv.at[i], asem.at[i])
        if i:
            plane_send[i - 1] = (own[i] + part_recv[i].astype(F32)).astype(BF16)
            send(plane_send.at[i - 1], plane_recv.at[i - 1], bsem.at[i - 1], (target * 2 + core, c))
        else:
            own[0] = own[0] + part_recv[0].astype(F32)

    acc[...] = nt(cot[:, pl.ds(pl.multiple_of(c * dz, dz), dz)], w_ref[...])
    w_plane(0)
    for step in range(1, n - 1):
        w_z(step)
        if step == 1:
            inter = nt(read_ref[...], inj_ref[...])
            for h in range(heads):
                spread = jnp.where(lower, cum_col[h] - cum_row[h], 0.0)
                weight = jnp.where(lower, jnp.exp(spread), 0.0)
                wts[h] = weight
                qts[h] = inter * weight * spread
                high, low = halves(jnp.exp(cum_col[h]) * read_ref[...].astype(F32))
                scal[h, :, :128] = high
                scal[h, :, 128:] = low
        w_use(step - 1)
        w_plane(step)
    w_use(n - 2)

    grad = acc[...].astype(BF16)
    grad_t = grad.astype(F32).T.astype(BF16)
    last = [cum_col[h][length - 1 : length, :] for h in range(heads)]
    pieces = []
    for h in range(heads):
        both = nn(grad_t[h * 128 : (h + 1) * 128], scal[h])
        pieces.append(both[:, :128] + both[:, 128:])
    before = (dp, lax.rem(c + n - 1, n))

    @pl.when(c == n - 1)
    def _():
        inc[...] = jnp.zeros_like(inc)

    for h in range(heads):
        chain_send[h] = pieces[h]
        send(chain_send.at[h], inc.at[h], chsem.at[h], before, c == n - 1)

    inject, read = inj_ref[...], read_ref[...]
    pair = pair_t = None
    rates = []
    through_sum = None
    for h in range(heads):
        ch = slice(h * 128, (h + 1) * 128)
        raw = nt(grad[:, ch], x_ref[:, ch])
        raw_t = nt(x_ref[:, ch], grad[:, ch])
        one, one_t = raw * wts[h], raw_t * wts_t[h]
        pair = one if pair is None else pair + one
        pair_t = one_t if pair_t is None else pair_t + one_t
        rate_row = fold(jnp.sum(raw * qts[h], axis=0, keepdims=True))
        high, low = halves(start_ref[h])
        through = jnp.exp(cum_col[h]) * (nn(grad[:, ch], high) + nn(grad[:, ch], low))
        through_sum = through if through_sum is None else through_sum + through
        rate_row = rate_row + jnp.sum(cum_col[h] * (through * read.astype(F32)), axis=0, keepdims=True)
        rates.append(rate_row)
    gread_ref[...] = nn(pair.astype(BF16), inject) + through_sum
    ginj_ref[...] = nn(pair_t.astype(BF16), read)

    for h in range(heads):
        @pl.when(c < n - 1)
        def _():
            arrived(inc.at[h], chsem.at[h])

        @pl.when((c < n - 1) & (c > 0))
        def _():
            chain_send[h] = chain_send[h] + jnp.exp(last[h]) * inc[h]

        send(chain_send.at[h], inc.at[h], chsem.at[h], before, (c < n - 1) & (c > 0))

    for i in range(chips - 1):
        arrived(plane_recv.at[i], bsem.at[i])
        own[0] = own[0] + plane_recv[i].astype(F32)
    for i in range(1, n):
        target = lax.rem(c + i, n)
        at = pl.ds(pl.multiple_of(target * rows, rows), rows)
        zsend[i - 1] = own[0, at, :].astype(BF16)
        send(zsend.at[i - 1], zrecv.at[i - 1], dsem.at[i - 1], (dp, target))

    rate_mine[...] = jnp.zeros_like(rate_mine)
    ginj = ginj_ref[...]
    for h in range(heads):
        ch = slice(h * 128, (h + 1) * 128)
        left = last[h] - cum_col[h]
        to_end = jnp.exp(left)
        high, low = halves(inc[h])
        entering = to_end * nt(inject, high)
        gi_ref[:, ch] = (nn(mix_t[h], grad[:, ch]) + entering).astype(BF16)
        reach = to_end * (nn(x_ref[:, ch], high) + nn(x_ref[:, ch], low))
        ginj = ginj + reach
        row = rates[h] + jnp.sum(left * (reach * inject.astype(F32)), axis=0, keepdims=True)
        row = row + (jnp.exp(last[h]) * last[h]) * jnp.sum(inc[h] * start_ref[h], axis=0, keepdims=True)
        rate_mine[h : h + 1, :] = row
    ginj_ref[...] = ginj

    for i in range(1, n):
        send(rate_mine, rate_z.at[i - 1], r1sem.at[i - 1], (dp, lax.rem(c + i, n)))
    total = rate_mine[...]
    for i in range(n - 1):
        arrived(rate_z.at[i], r1sem.at[i])
        total = total + rate_z[i]
    rate_mid[...] = total
    for i in range(1, dps):
        send(rate_mid, rate_dp.at[i - 1], r2sem.at[i - 1], (lax.rem(dp + i, dps), c))

    at = pl.ds(pl.multiple_of(c * rows, rows), rows)
    result = own[0, at, :]
    for i in range(n - 1):
        arrived(zrecv.at[i], dsem.at[i])
        result = result + zrecv[i].astype(F32)
    gw_ref[...] = result

    for i in range(dps - 1):
        arrived(rate_dp.at[i], r2sem.at[i])
        total = total + rate_dp[i]
    rate_out[...] = total

    for copy, cond in sent:
        if cond is None:
            copy.wait_send()
        else:
            pl.when(cond)(lambda: copy.wait_send())


def local(n, dps, cotangent, out_weight, head_input, injector, readout, decay_code, decay_rate, start_state):
    length, width = cotangent.shape[1:]
    channels, dz = out_weight.shape
    heads = decay_rate.shape[0]
    chips = dps // 2
    rows, cols = channels // n, width // dps
    code = decay_code[0]
    parts = jnp.concatenate([code // 256, code % 256], axis=1).astype(BF16)
    code_col = jnp.pad(parts, ((0, 0), (0, 128 - 2 * heads)))
    code_row = jnp.pad(parts.T, ((0, 16 - 2 * heads), (0, 0)))
    sends = 2 + 2 * (n - 2) + 6 * (n - 1) + chips + (chips - 1) + 2 * heads + 2 * (n - 1) + (dps - 1)
    vmem = pl.BlockSpec(memory_space=pltpu.VMEM)
    dma = pltpu.SemaphoreType.DMA
    gi, ginj, gread, gw, rate = pl.pallas_call(
        functools.partial(kernel, n, dps),
        out_shape=(
            jax.ShapeDtypeStruct((length, channels), BF16),
            jax.ShapeDtypeStruct((length, 128), F32),
            jax.ShapeDtypeStruct((length, 128), F32),
            jax.ShapeDtypeStruct((rows, cols), F32),
            jax.ShapeDtypeStruct((8, 128), F32),
        ),
        in_specs=[pl.BlockSpec(memory_space=pltpu.SMEM), pl.BlockSpec(memory_space=pl.ANY)] + [vmem] * 7,
        out_specs=(vmem,) * 5,
        scratch_shapes=[
            pltpu.VMEM((length, width), BF16),
            pltpu.VMEM((2, n - 1, channels, dz), BF16),
            pltpu.VMEM((length, channels), F32),
            pltpu.VMEM((chips, channels, cols), F32),
            pltpu.VMEM((chips, channels, cols), BF16),
            pltpu.VMEM((chips, channels, cols), BF16),
            pltpu.VMEM((chips - 1, channels, cols), BF16),
            pltpu.VMEM((chips - 1, channels, cols), BF16),
            pltpu.VMEM((n - 1, rows, cols), BF16),
            pltpu.VMEM((n - 1, rows, cols), BF16),
            pltpu.VMEM((channels, length), BF16),
            pltpu.VMEM((heads, length, length), BF16),
            pltpu.VMEM((heads, length, length), F32),
            pltpu.VMEM((heads, length, length), F32),
            pltpu.VMEM((heads, length, length), F32),
            pltpu.VMEM((heads, length, 256), BF16),
            pltpu.VMEM((heads, 128, 128), F32),
            pltpu.VMEM((heads, 128, 128), F32),
            pltpu.VMEM((n - 1, 8, 128), F32),
            pltpu.VMEM((dps - 1, 8, 128), F32),
            pltpu.VMEM((8, 128), F32),
            pltpu.VMEM((8, 128), F32),
            dma((4,)),
            dma((sends,)),
            dma((2, n - 1)),
            dma((2, n - 1)),
            dma((2, n - 1, 2)),
            dma((chips,)),
            dma((chips - 1,)),
            dma((n - 1,)),
            dma((heads,)),
            dma((n - 1,)),
            dma((dps - 1,)),
        ],
        compiler_params=pltpu.CompilerParams(
            collective_id=0, has_side_effects=True, vmem_limit_bytes=60 * 1024 * 1024
        ),
        cost_estimate=pl.CostEstimate(flops=10**10, bytes_accessed=2 * 10**7, transcendentals=10**6),
    )(
        decay_rate, cotangent[0], out_weight, head_input[0], injector[0], readout[0],
        code_col, code_row, start_state[0, 0],
    )
    tokens_all = length * dps * n
    return gi[None], ginj[None], gread[None], gw, jnp.sum(rate, axis=1)[:heads] / tokens_all


def solution(mesh):
    n, dps = mesh.shape["ctx"], mesh.shape["dp"]
    in_specs = (
        P("dp", "ctx", None),
        P(None, "ctx"),
        P("dp", "ctx", None),
        P("dp", "ctx", None),
        P("dp", "ctx", None),
        P("dp", "ctx", None),
        P(),
        P("dp", "ctx", None, None, None),
    )
    out_specs = (
        P("dp", "ctx", None),
        P("dp", "ctx", None),
        P("dp", "ctx", None),
        P("ctx", "dp"),
        P(),
    )
    return jax.shard_map(
        functools.partial(local, n, dps), mesh=mesh, in_specs=in_specs, out_specs=out_specs, check_vma=False
    )
```

```python
import functools

import jax
import jax.numpy as jnp
from jax import lax
from jax.experimental import pallas as pl
from jax.experimental.pallas import tpu as pltpu
from jax.sharding import PartitionSpec as P

F32, BF16 = jnp.float32, jnp.bfloat16
MESH = pl.DeviceIdType.MESH


def nn(a, b):
    return lax.dot_general(a, b, (((1,), (0,)), ((), ())), preferred_element_type=F32)


def nt(a, b):
    return lax.dot_general(a, b, (((1,), (1,)), ((), ())), preferred_element_type=F32)


def halves(value):
    high = value.astype(BF16)
    return high, (value - high.astype(F32)).astype(BF16)


def fold(row):
    total = row[:, :128]
    for at in range(128, row.shape[1], 128):
        total = total + row[:, at : at + 128]
    return total


def kernel(
    n, dps,
    rate_ref, cot_hbm, w_ref, x_ref, inj_ref, read_ref, codecol_ref, start_ref,
    gi_ref, ginj_ref, gread_ref, gw_ref, rate_out,
    cot, wslot, acc, own, part_send, part_recv, plane_send, plane_recv, zsend, zrecv,
    fwd_t, mix_t, wts, wts_t, qts, scal, inc, chain_send, rate_z, rate_dp, rate_mine, rate_mid,
    cot_sem, send_sem, zsem, psem, csem, asem, bsem, dsem, chsem, r1sem, r2sem,
):
    length, heads = x_ref.shape[0], start_ref.shape[0]
    dz = w_ref.shape[1]
    chips = dps // 2
    rows, cols = gw_ref.shape
    dp, c = lax.axis_index("dp"), lax.axis_index("ctx")
    chip, core = lax.div(dp, 2), lax.rem(dp, 2)
    partner = (chip * 2 + 1 - core, c)
    quarter = w_ref.shape[0] // 4
    sent = []
    counter = [0]

    def send(src, dst, recv_sem, device, cond=None):
        index = counter[0]
        counter[0] += 1
        copy = pltpu.make_async_remote_copy(
            src_ref=src, dst_ref=dst, send_sem=send_sem.at[index], recv_sem=recv_sem,
            device_id=device, device_id_type=MESH,
        )
        sent.append((copy, cond))
        if cond is None:
            copy.start()
        else:
            pl.when(cond)(lambda: copy.start())

    def arrived(dst, recv_sem):
        pltpu.make_async_copy(dst, dst, recv_sem).wait()

    loads = []
    for i in range(4):
        r = pl.ds(i * (length // 4), length // 4)
        load = pltpu.make_async_copy(cot_hbm.at[r], cot.at[r], cot_sem.at[i])
        load.start()
        loads.append(load)

    barrier = pltpu.get_barrier_semaphore()
    for i in range(1, dps):
        pl.semaphore_signal(barrier, inc=1, device_id=(lax.rem(dp + i, dps), c), device_id_type=MESH)
    for i in range(1, n):
        pl.semaphore_signal(barrier, inc=1, device_id=(dp, lax.rem(c + i, n)), device_id_type=MESH)
    pl.semaphore_wait(barrier, dps + n - 2)

    def shard_place(shard):
        par = lax.rem(shard, 2)
        bit = lax.rem(chip, 2) * (1 - par) + lax.rem(lax.div(chip, 2), 2) * par
        peer = chip + (1 - 2 * bit) * (1 + par)
        return bit, peer

    def q_rows(k, bit):
        return pl.ds(pl.multiple_of((2 * k + bit) * quarter, quarter), quarter)

    bit, _ = shard_place(c)
    mine = q_rows(core, bit)
    send(w_ref.at[mine], wslot.at[0, 0, mine], zsem.at[0, 0], (dp, lax.rem(c + 1, n)), c + 1 < n)
    send(w_ref.at[mine], wslot.at[1, 0, mine], zsem.at[1, 0], (dp, lax.rem(c + n - 1, n)), c > 0)

    def shard_of(way, step):
        return (c - 1 - step, c - 1 - step >= 0) if way == 0 else (c + 1 + step, c + 1 + step < n)

    def w_z(step):
        for way in range(2):
            shard, valid = shard_of(way, step)
            shard = lax.rem(shard + n, n)
            bit, peer = shard_place(shard)
            here = q_rows(core, bit)
            slot = wslot.at[way, step, here]
            pl.when(valid)(lambda: arrived(slot, zsem.at[way, step]))
            if step + 1 < n - 1:
                if way == 0:
                    send(slot, wslot.at[way, step + 1, here], zsem.at[way, step + 1],
                         (dp, lax.rem(c + 1, n)), valid & (c + 1 < n))
                else:
                    send(slot, wslot.at[way, step + 1, here], zsem.at[way, step + 1],
                         (dp, lax.rem(c + n - 1, n)), valid & (c > 0))
            send(slot, slot, psem.at[way, step], (peer * 2 + core, c), valid)
            send(slot, slot, csem.at[way, step, 0], partner, valid)

    def w_plane(step):
        for way in range(2):
            shard, valid = shard_of(way, step)
            shard = lax.rem(shard + n, n)
            bit, _ = shard_place(shard)
            slot = wslot.at[way, step, q_rows(core, 1 - bit)]
            pl.when(valid)(lambda: arrived(slot, psem.at[way, step]))
            send(slot, slot, csem.at[way, step, 1], partner, valid)

    def w_use(step):
        for way in range(2):
            shard, valid = shard_of(way, step)
            shard = lax.rem(shard + n, n)
            bit, _ = shard_place(shard)

            @pl.when(valid)
            def _():
                for which in range(2):
                    there = bit if which == 0 else 1 - bit
                    arrived(wslot.at[way, step, q_rows(1 - core, there)], csem.at[way, step, which])
                at = pl.ds(pl.multiple_of(shard * dz, dz), dz)
                acc[...] += nt(cot[:, at], wslot[way, step])

    row_at = lax.broadcasted_iota(jnp.int32, (length, length), 0)
    col_at = lax.broadcasted_iota(jnp.int32, (length, length), 1)
    lower = row_at >= col_at
    upper = col_at >= row_at
    col_sum = nn(jnp.where(lower, 1.0, 0.0).astype(BF16), codecol_ref[...])
    row_sum = col_sum.T
    inter_t = nt(inj_ref[...], read_ref[...])
    x_t = x_ref[...].astype(F32).T.astype(BF16)
    cum_col, cum_row = [], []
    for h in range(heads):
        ch = slice(h * 128, (h + 1) * 128)
        rate = rate_ref[h]
        cc = -rate * (256.0 * col_sum[:, h : h + 1] + col_sum[:, heads + h : heads + h + 1])
        cr = -rate * (256.0 * row_sum[h : h + 1] + row_sum[heads + h : heads + h + 1])
        cum_col.append(cc)
        cum_row.append(cr)
        w_t = jnp.where(upper, jnp.exp(jnp.where(upper, cr - cc, 0.0)), 0.0)
        wts_t[h] = w_t
        mixed = (inter_t * w_t).astype(BF16)
        mix_t[h] = mixed
        high, low = halves(start_ref[h])
        carried = nt(high, read_ref[...]) + nt(low, read_ref[...])
        fwd_t[ch, :] = (nn(x_t[ch], mixed) + jnp.exp(cr) * carried).astype(BF16)

    for load in loads:
        load.wait()

    def block(chip_at, core_at):
        at = pl.ds(pl.multiple_of((chip_at * 2 + core_at) * cols, cols), cols)
        return nn(fwd_t[...], cot[:, at])

    levels = chips.bit_length() - 1
    bits = [lax.rem(lax.div(chip, 1 << k), 2) for k in range(levels)]

    def chip_across(offset):
        return chip + sum(((1 << k) * (1 - 2 * bits[k]) for k in range(levels) if offset >> k & 1), 0)

    half = fwd_t.shape[0] // 2
    ways = (list(range(levels)), list(range(levels))[::-1])

    def leaving(way, level):
        keys = ways[way]
        return [r for r in range(chips) if r >> keys[level] & 1 and not any(r >> keys[k] & 1 for k in range(level))]

    def plane_out(way, level, r):
        bit_at = 1 << ways[way][level]
        at = slice(way * half, (way + 1) * half)
        plane_send[way, r - 1] = own[r, at].astype(BF16)
        send(plane_send.at[way, r - 1], plane_recv.at[way, r - 1], bsem.at[way, r - 1],
             (chip_across(bit_at) * 2 + core, c))

    def plane_in(level):
        for way in range(2):
            bit_at = 1 << ways[way][level]
            at = slice(way * half, (way + 1) * half)
            for r in leaving(way, level):
                arrived(plane_recv.at[way, r - 1], bsem.at[way, r - 1])
                own[r - bit_at, at] = own[r - bit_at, at] + plane_recv[way, r - 1].astype(F32)
            if level + 1 < levels:
                for r in leaving(way, level + 1):
                    plane_out(way, level + 1, r)

    first = [r for r in range(1, chips) if r & 1 and r >> (levels - 1) & 1]
    order = first + [r for r in range(chips - 1, -1, -1) if r not in first]
    for r in order:
        part_send[r] = block(chip_across(r), 1 - core).astype(BF16)
        send(part_send.at[r], part_recv.at[r], asem.at[r], partner)
    w_z(0)
    for r in order:
        mine_too = block(chip_across(r), core)
        arrived(part_recv.at[r], asem.at[r])
        own[r] = mine_too + part_recv[r].astype(F32)
        for way in range(2):
            if r in leaving(way, 0):
                plane_out(way, 0, r)

    w_plane(0)
    acc[...] = nt(cot[:, pl.ds(pl.multiple_of(c * dz, dz), dz)], w_ref[...])
    for step in range(1, n - 1):
        w_z(step)
        if step == 1:
            inter = nt(read_ref[...], inj_ref[...])
            for h in range(heads):
                spread = jnp.where(lower, cum_col[h] - cum_row[h], 0.0)
                weight = jnp.where(lower, jnp.exp(spread), 0.0)
                wts[h] = weight
                qts[h] = inter * weight * spread
                high, low = halves(jnp.exp(cum_col[h]) * read_ref[...].astype(F32))
                scal[h, :, :128] = high
                scal[h, :, 128:] = low
            for level in range(levels - 1):
                plane_in(level)
        w_use(step - 1)
        w_plane(step)
    plane_in(levels - 1)
    for i in range(1, n):
        target = lax.rem(c + i, n)
        at = pl.ds(pl.multiple_of(target * rows, rows), rows)
        zsend[i - 1] = own[0, at, :].astype(BF16)
        send(zsend.at[i - 1], zrecv.at[i - 1], dsem.at[i - 1], (dp, target))
    w_use(n - 2)

    grad = acc[...].astype(BF16)
    grad_t = grad.astype(F32).T.astype(BF16)
    last = [cum_col[h][length - 1 : length, :] for h in range(heads)]
    pieces = []
    for h in range(heads):
        both = nn(grad_t[h * 128 : (h + 1) * 128], scal[h])
        pieces.append(both[:, :128] + both[:, 128:])
    before = (dp, lax.rem(c + n - 1, n))

    @pl.when(c == n - 1)
    def _():
        inc[...] = jnp.zeros_like(inc)

    for h in range(heads):
        chain_send[h] = pieces[h]
        send(chain_send.at[h], inc.at[h], chsem.at[h], before, c == n - 1)

    inject, read = inj_ref[...], read_ref[...]
    pair = pair_t = None
    rates = []
    through_sum = None
    for h in range(heads):
        ch = slice(h * 128, (h + 1) * 128)
        raw = nt(grad[:, ch], x_ref[:, ch])
        raw_t = nt(x_ref[:, ch], grad[:, ch])
        one, one_t = raw * wts[h], raw_t * wts_t[h]
        pair = one if pair is None else pair + one
        pair_t = one_t if pair_t is None else pair_t + one_t
        rate_row = fold(jnp.sum(raw * qts[h], axis=0, keepdims=True))
        high, low = halves(start_ref[h])
        through = jnp.exp(cum_col[h]) * (nn(grad[:, ch], high) + nn(grad[:, ch], low))
        through_sum = through if through_sum is None else through_sum + through
        rate_row = rate_row + jnp.sum(cum_col[h] * (through * read.astype(F32)), axis=0, keepdims=True)
        rates.append(rate_row)
    gread_ref[...] = nn(pair.astype(BF16), inject) + through_sum
    ginj_ref[...] = nn(pair_t.astype(BF16), read)

    for h in range(heads):
        @pl.when(c < n - 1)
        def _():
            arrived(inc.at[h], chsem.at[h])

        @pl.when((c < n - 1) & (c > 0))
        def _():
            chain_send[h] = chain_send[h] + jnp.exp(last[h]) * inc[h]

        send(chain_send.at[h], inc.at[h], chsem.at[h], before, (c < n - 1) & (c > 0))

    rate_mine[...] = jnp.zeros_like(rate_mine)
    ginj = ginj_ref[...]
    for h in range(heads):
        ch = slice(h * 128, (h + 1) * 128)
        left = last[h] - cum_col[h]
        to_end = jnp.exp(left)
        high, low = halves(inc[h])
        entering = to_end * nt(inject, high)
        gi_ref[:, ch] = (nn(mix_t[h], grad[:, ch]) + entering).astype(BF16)
        reach = to_end * (nn(x_ref[:, ch], high) + nn(x_ref[:, ch], low))
        ginj = ginj + reach
        row = rates[h] + jnp.sum(left * (reach * inject.astype(F32)), axis=0, keepdims=True)
        row = row + (jnp.exp(last[h]) * last[h]) * jnp.sum(inc[h] * start_ref[h], axis=0, keepdims=True)
        rate_mine[h : h + 1, :] = row
    ginj_ref[...] = ginj

    for i in range(1, n):
        send(rate_mine, rate_z.at[i - 1], r1sem.at[i - 1], (dp, lax.rem(c + i, n)))
    total = rate_mine[...]
    for i in range(n - 1):
        arrived(rate_z.at[i], r1sem.at[i])
        total = total + rate_z[i]
    rate_mid[...] = total
    for i in range(1, dps):
        send(rate_mid, rate_dp.at[i - 1], r2sem.at[i - 1], (lax.rem(dp + i, dps), c))

    at = pl.ds(pl.multiple_of(c * rows, rows), rows)
    result = own[0, at, :]
    for i in range(n - 1):
        arrived(zrecv.at[i], dsem.at[i])
        result = result + zrecv[i].astype(F32)
    gw_ref[...] = result

    for i in range(dps - 1):
        arrived(rate_dp.at[i], r2sem.at[i])
        total = total + rate_dp[i]
    whole = jnp.sum(total, axis=1, keepdims=True) / (length * dps * n)
    rate_out[...] = jnp.broadcast_to(whole, rate_out.shape)

    for copy, cond in sent:
        if cond is None:
            copy.wait_send()
        else:
            pl.when(cond)(lambda: copy.wait_send())


def hand_over(*refs):
    copies = [pltpu.make_async_copy(refs[i], refs[4 + i], refs[8].at[i]) for i in range(4)]
    for copy in copies:
        copy.start()
    for copy in copies:
        copy.wait()


def local(n, dps, cotangent, out_weight, head_input, injector, readout, decay_code, decay_rate, start_state):
    length, width = cotangent.shape[1:]
    channels, dz = out_weight.shape
    heads = decay_rate.shape[0]
    chips = dps // 2
    rows, cols = channels // n, width // dps
    code = decay_code[0]
    parts = jnp.concatenate([code // 256, code % 256], axis=1).astype(BF16)
    code_col = jnp.pad(parts, ((0, 0), (0, 128 - 2 * heads)))
    sends = 2 + 2 * (n - 2) + 6 * (n - 1) + chips + 2 * (chips - 1) + 2 * heads + 2 * (n - 1) + (dps - 1)
    vmem = pl.BlockSpec(memory_space=pltpu.VMEM)
    dma = pltpu.SemaphoreType.DMA
    gi, ginj, gread, gw, rate = pl.pallas_call(
        functools.partial(kernel, n, dps),
        out_shape=(
            jax.ShapeDtypeStruct((length, channels), BF16),
            jax.ShapeDtypeStruct((length, 128), F32),
            jax.ShapeDtypeStruct((length, 128), F32),
            jax.ShapeDtypeStruct((rows, cols), F32),
            jax.ShapeDtypeStruct((8, 128), F32),
        ),
        in_specs=[pl.BlockSpec(memory_space=pltpu.SMEM), pl.BlockSpec(memory_space=pl.ANY)] + [vmem] * 6,
        out_specs=(vmem,) * 5,
        scratch_shapes=[
            pltpu.VMEM((length, width), BF16),
            pltpu.VMEM((2, n - 1, channels, dz), BF16),
            pltpu.VMEM((length, channels), F32),
            pltpu.VMEM((chips, channels, cols), F32),
            pltpu.VMEM((chips, channels, cols), BF16),
            pltpu.VMEM((chips, channels, cols), BF16),
            pltpu.VMEM((2, chips - 1, channels // 2, cols), BF16),
            pltpu.VMEM((2, chips - 1, channels // 2, cols), BF16),
            pltpu.VMEM((n - 1, rows, cols), BF16),
            pltpu.VMEM((n - 1, rows, cols), BF16),
            pltpu.VMEM((channels, length), BF16),
            pltpu.VMEM((heads, length, length), BF16),
            pltpu.VMEM((heads, length, length), F32),
            pltpu.VMEM((heads, length, length), F32),
            pltpu.VMEM((heads, length, length), F32),
            pltpu.VMEM((heads, length, 256), BF16),
            pltpu.VMEM((heads, 128, 128), F32),
            pltpu.VMEM((heads, 128, 128), F32),
            pltpu.VMEM((n - 1, 8, 128), F32),
            pltpu.VMEM((dps - 1, 8, 128), F32),
            pltpu.VMEM((8, 128), F32),
            pltpu.VMEM((8, 128), F32),
            dma((4,)),
            dma((sends,)),
            dma((2, n - 1)),
            dma((2, n - 1)),
            dma((2, n - 1, 2)),
            dma((chips,)),
            dma((2, chips - 1)),
            dma((n - 1,)),
            dma((heads,)),
            dma((n - 1,)),
            dma((dps - 1,)),
        ],
        compiler_params=pltpu.CompilerParams(
            collective_id=0, has_side_effects=True, vmem_limit_bytes=60 * 1024 * 1024
        ),
        cost_estimate=pl.CostEstimate(flops=10**10, bytes_accessed=2 * 10**7, transcendentals=10**6),
    )(
        decay_rate, cotangent[0], out_weight, head_input[0], injector[0], readout[0],
        code_col, start_state[0, 0],
    )
    anywhere = pl.BlockSpec(memory_space=pl.ANY)
    results = (gi, ginj, gread, gw)
    gi, ginj, gread, gw = pl.pallas_call(
        hand_over,
        out_shape=tuple(jax.ShapeDtypeStruct(part.shape, part.dtype) for part in results),
        in_specs=[anywhere] * 4,
        out_specs=(anywhere,) * 4,
        scratch_shapes=[dma((4,))],
    )(*results)
    return gi[None], ginj[None], gread[None], gw, rate[:heads, 0]


def solution(mesh):
    n, dps = mesh.shape["ctx"], mesh.shape["dp"]
    in_specs = (
        P("dp", "ctx", None),
        P(None, "ctx"),
        P("dp", "ctx", None),
        P("dp", "ctx", None),
        P("dp", "ctx", None),
        P("dp", "ctx", None),
        P(),
        P("dp", "ctx", None, None, None),
    )
    out_specs = (
        P("dp", "ctx", None),
        P("dp", "ctx", None),
        P("dp", "ctx", None),
        P("ctx", "dp"),
        P(),
    )
    return jax.shard_map(
        functools.partial(local, n, dps), mesh=mesh, in_specs=in_specs, out_specs=out_specs, check_vma=False
    )
```

```python
import functools

import jax
import jax.numpy as jnp
from jax import lax
from jax.experimental import pallas as pl
from jax.experimental.pallas import tpu as pltpu
from jax.sharding import PartitionSpec as P

F32, BF16 = jnp.float32, jnp.bfloat16
MESH = pl.DeviceIdType.MESH


def nn(a, b):
    return lax.dot_general(a, b, (((1,), (0,)), ((), ())), preferred_element_type=F32)


def nt(a, b):
    return lax.dot_general(a, b, (((1,), (1,)), ((), ())), preferred_element_type=F32)


def halves(value):
    high = value.astype(BF16)
    return high, (value - high.astype(F32)).astype(BF16)


def fold(row):
    total = row[:, :128]
    for at in range(128, row.shape[1], 128):
        total = total + row[:, at : at + 128]
    return total


def kernel(
    n, dps,
    rate_ref, cot_hbm, w_ref, x_ref, inj_ref, read_ref, codecol_ref, start_ref,
    gi_ref, ginj_ref, gread_ref, gw_ref, rate_out,
    cot, wslot, acc, own, part_send, part_recv, plane_send, plane_recv, zsend, zrecv,
    fwd_t, mix_t, wts, wts_t, qts, scal, inc, chain_send, rate_z, rate_dp, rate_mine, rate_mid,
    cot_sem, send_sem, zsem, psem, csem, asem, bsem, dsem, chsem, r1sem, r2sem,
):
    length, heads = x_ref.shape[0], start_ref.shape[0]
    dz = w_ref.shape[1]
    chips = dps // 2
    rows, cols = gw_ref.shape
    dp, c = lax.axis_index("dp"), lax.axis_index("ctx")
    chip, core = lax.div(dp, 2), lax.rem(dp, 2)
    partner = (chip * 2 + 1 - core, c)
    quarter = w_ref.shape[0] // 4
    sent = []
    counter = [0]

    def send(src, dst, recv_sem, device, cond=None):
        index = counter[0]
        counter[0] += 1
        copy = pltpu.make_async_remote_copy(
            src_ref=src, dst_ref=dst, send_sem=send_sem.at[index], recv_sem=recv_sem,
            device_id=device, device_id_type=MESH,
        )
        sent.append((copy, cond))
        if cond is None:
            copy.start()
        else:
            pl.when(cond)(lambda: copy.start())

    def arrived(dst, recv_sem):
        pltpu.make_async_copy(dst, dst, recv_sem).wait()

    loads = []
    for i in range(4):
        r = pl.ds(i * (length // 4), length // 4)
        load = pltpu.make_async_copy(cot_hbm.at[r], cot.at[r], cot_sem.at[i])
        load.start()
        loads.append(load)

    barrier = pltpu.get_barrier_semaphore()
    for i in range(1, dps):
        pl.semaphore_signal(barrier, inc=1, device_id=(lax.rem(dp + i, dps), c), device_id_type=MESH)
    for i in range(1, n):
        pl.semaphore_signal(barrier, inc=1, device_id=(dp, lax.rem(c + i, n)), device_id_type=MESH)
    pl.semaphore_wait(barrier, dps + n - 2)

    def shard_place(shard):
        par = lax.rem(shard, 2)
        bit = lax.rem(chip, 2) * (1 - par) + lax.rem(lax.div(chip, 2), 2) * par
        peer = chip + (1 - 2 * bit) * (1 + par)
        return bit, peer

    def q_rows(k, bit):
        return pl.ds(pl.multiple_of((2 * k + bit) * quarter, quarter), quarter)

    bit, _ = shard_place(c)
    mine = q_rows(core, bit)
    send(w_ref.at[mine], wslot.at[0, 0, mine], zsem.at[0, 0], (dp, lax.rem(c + 1, n)), c + 1 < n)
    send(w_ref.at[mine], wslot.at[1, 0, mine], zsem.at[1, 0], (dp, lax.rem(c + n - 1, n)), c > 0)

    def shard_of(way, step):
        return (c - 1 - step, c - 1 - step >= 0) if way == 0 else (c + 1 + step, c + 1 + step < n)

    def w_z(step):
        for way in range(2):
            shard, valid = shard_of(way, step)
            shard = lax.rem(shard + n, n)
            bit, peer = shard_place(shard)
            here = q_rows(core, bit)
            slot = wslot.at[way, step, here]
            pl.when(valid)(lambda: arrived(slot, zsem.at[way, step]))
            if step + 1 < n - 1:
                if way == 0:
                    send(slot, wslot.at[way, step + 1, here], zsem.at[way, step + 1],
                         (dp, lax.rem(c + 1, n)), valid & (c + 1 < n))
                else:
                    send(slot, wslot.at[way, step + 1, here], zsem.at[way, step + 1],
                         (dp, lax.rem(c + n - 1, n)), valid & (c > 0))
            send(slot, slot, psem.at[way, step], (peer * 2 + core, c), valid)
            send(slot, slot, csem.at[way, step, 0], partner, valid)

    def w_plane(step):
        for way in range(2):
            shard, valid = shard_of(way, step)
            shard = lax.rem(shard + n, n)
            bit, _ = shard_place(shard)
            slot = wslot.at[way, step, q_rows(core, 1 - bit)]
            pl.when(valid)(lambda: arrived(slot, psem.at[way, step]))
            send(slot, slot, csem.at[way, step, 1], partner, valid)

    def w_use(step):
        for way in range(2):
            shard, valid = shard_of(way, step)
            shard = lax.rem(shard + n, n)
            bit, _ = shard_place(shard)

            @pl.when(valid)
            def _():
                for which in range(2):
                    there = bit if which == 0 else 1 - bit
                    arrived(wslot.at[way, step, q_rows(1 - core, there)], csem.at[way, step, which])
                at = pl.ds(pl.multiple_of(shard * dz, dz), dz)
                acc[...] += nt(cot[:, at], wslot[way, step])

    row_at = lax.broadcasted_iota(jnp.int32, (length, length), 0)
    col_at = lax.broadcasted_iota(jnp.int32, (length, length), 1)
    lower = row_at >= col_at
    upper = col_at >= row_at
    col_sum = nn(jnp.where(lower, 1.0, 0.0).astype(BF16), codecol_ref[...])
    row_sum = col_sum.T
    inter_t = nt(inj_ref[...], read_ref[...])
    x_t = x_ref[...].astype(F32).T.astype(BF16)
    cum_col, cum_row = [], []
    for h in range(heads):
        ch = slice(h * 128, (h + 1) * 128)
        rate = rate_ref[h]
        cc = -rate * (256.0 * col_sum[:, h : h + 1] + col_sum[:, heads + h : heads + h + 1])
        cr = -rate * (256.0 * row_sum[h : h + 1] + row_sum[heads + h : heads + h + 1])
        cum_col.append(cc)
        cum_row.append(cr)
        w_t = jnp.where(upper, jnp.exp(jnp.where(upper, cr - cc, 0.0)), 0.0)
        wts_t[h] = w_t
        mixed = (inter_t * w_t).astype(BF16)
        mix_t[h] = mixed
        high, low = halves(start_ref[h])
        carried = nt(high, read_ref[...]) + nt(low, read_ref[...])
        fwd_t[ch, :] = (nn(x_t[ch], mixed) + jnp.exp(cr) * carried).astype(BF16)

    for load in loads:
        load.wait()

    def block(chip_at, core_at):
        at = pl.ds(pl.multiple_of((chip_at * 2 + core_at) * cols, cols), cols)
        return nn(fwd_t[...], cot[:, at])

    levels = chips.bit_length() - 1
    bits = [lax.rem(lax.div(chip, 1 << k), 2) for k in range(levels)]

    def chip_across(offset):
        return chip + sum(((1 << k) * (1 - 2 * bits[k]) for k in range(levels) if offset >> k & 1), 0)

    half = fwd_t.shape[0] // 2
    ways = (list(range(levels)), list(range(levels))[::-1])

    def leaving(way, level):
        keys = ways[way]
        return [r for r in range(chips) if r >> keys[level] & 1 and not any(r >> keys[k] & 1 for k in range(level))]

    def plane_out(way, level, r):
        bit_at = 1 << ways[way][level]
        at = slice(way * half, (way + 1) * half)
        plane_send[way, r - 1] = own[r, at].astype(BF16)
        send(plane_send.at[way, r - 1], plane_recv.at[way, r - 1], bsem.at[way, r - 1],
             (chip_across(bit_at) * 2 + core, c))

    def plane_in(level):
        for way in range(2):
            bit_at = 1 << ways[way][level]
            at = slice(way * half, (way + 1) * half)
            for r in leaving(way, level):
                arrived(plane_recv.at[way, r - 1], bsem.at[way, r - 1])
                own[r - bit_at, at] = own[r - bit_at, at] + plane_recv[way, r - 1].astype(F32)
            if level + 1 < levels:
                for r in leaving(way, level + 1):
                    plane_out(way, level + 1, r)

    first = [r for r in range(1, chips) if r & 1 and r >> (levels - 1) & 1]
    order = first + [r for r in range(chips - 1, -1, -1) if r not in first]
    for r in order:
        part_send[r] = block(chip_across(r), 1 - core).astype(BF16)
        send(part_send.at[r], part_recv.at[r], asem.at[r], partner)
    w_z(0)
    for r in order:
        mine_too = block(chip_across(r), core)
        arrived(part_recv.at[r], asem.at[r])
        own[r] = mine_too + part_recv[r].astype(F32)
        for way in range(2):
            if r in leaving(way, 0):
                plane_out(way, 0, r)

    w_plane(0)
    acc[...] = nt(cot[:, pl.ds(pl.multiple_of(c * dz, dz), dz)], w_ref[...])
    for step in range(1, n - 1):
        w_z(step)
        if step == 1:
            inter = nt(read_ref[...], inj_ref[...])
            for h in range(heads):
                spread = jnp.where(lower, cum_col[h] - cum_row[h], 0.0)
                weight = jnp.where(lower, jnp.exp(spread), 0.0)
                wts[h] = weight
                qts[h] = inter * weight * spread
                high, low = halves(jnp.exp(cum_col[h]) * read_ref[...].astype(F32))
                scal[h, :, :128] = high
                scal[h, :, 128:] = low
        if step < n - 2:
            w_plane(step)
        w_use(step - 1)
    for level in range(levels - 1):
        plane_in(level)
    w_plane(n - 2)
    w_use(n - 2)

    grad = acc[...].astype(BF16)
    grad_t = grad.astype(F32).T.astype(BF16)
    last = [cum_col[h][length - 1 : length, :] for h in range(heads)]
    pieces = []
    for h in range(heads):
        both = nn(grad_t[h * 128 : (h + 1) * 128], scal[h])
        pieces.append(both[:, :128] + both[:, 128:])
    before = (dp, lax.rem(c + n - 1, n))

    @pl.when(c == n - 1)
    def _():
        inc[...] = jnp.zeros_like(inc)

    for h in range(heads):
        chain_send[h] = pieces[h]
        send(chain_send.at[h], inc.at[h], chsem.at[h], before, c == n - 1)

    inject, read = inj_ref[...], read_ref[...]
    pair = pair_t = None
    rates = []
    through_sum = None
    for h in range(heads):
        ch = slice(h * 128, (h + 1) * 128)
        raw = nt(grad[:, ch], x_ref[:, ch])
        raw_t = nt(x_ref[:, ch], grad[:, ch])
        one, one_t = raw * wts[h], raw_t * wts_t[h]
        pair = one if pair is None else pair + one
        pair_t = one_t if pair_t is None else pair_t + one_t
        rate_row = fold(jnp.sum(raw * qts[h], axis=0, keepdims=True))
        high, low = halves(start_ref[h])
        through = jnp.exp(cum_col[h]) * (nn(grad[:, ch], high) + nn(grad[:, ch], low))
        through_sum = through if through_sum is None else through_sum + through
        rate_row = rate_row + jnp.sum(cum_col[h] * (through * read.astype(F32)), axis=0, keepdims=True)
        rates.append(rate_row)
    gread_ref[...] = nn(pair.astype(BF16), inject) + through_sum
    ginj_ref[...] = nn(pair_t.astype(BF16), read)
    for h in range(heads):
        ch = slice(h * 128, (h + 1) * 128)
        acc[:, ch] = nn(mix_t[h], grad[:, ch])
    plane_in(levels - 1)
    for i in range(1, n):
        target = lax.rem(c + i, n)
        at = pl.ds(pl.multiple_of(target * rows, rows), rows)
        zsend[i - 1] = own[0, at, :].astype(BF16)
        send(zsend.at[i - 1], zrecv.at[i - 1], dsem.at[i - 1], (dp, target))

    for h in range(heads):
        @pl.when(c < n - 1)
        def _():
            arrived(inc.at[h], chsem.at[h])

        @pl.when((c < n - 1) & (c > 0))
        def _():
            chain_send[h] = chain_send[h] + jnp.exp(last[h]) * inc[h]

        send(chain_send.at[h], inc.at[h], chsem.at[h], before, (c < n - 1) & (c > 0))

    rate_mine[...] = jnp.zeros_like(rate_mine)
    reached = []
    for h in range(heads):
        ch = slice(h * 128, (h + 1) * 128)
        left = last[h] - cum_col[h]
        high, low = halves(inc[h])
        reach = jnp.exp(left) * (nn(x_ref[:, ch], high) + nn(x_ref[:, ch], low))
        reached.append(reach)
        row = rates[h] + jnp.sum(left * (reach * inject.astype(F32)), axis=0, keepdims=True)
        row = row + (jnp.exp(last[h]) * last[h]) * jnp.sum(inc[h] * start_ref[h], axis=0, keepdims=True)
        rate_mine[h : h + 1, :] = row
    for i in range(1, n):
        send(rate_mine, rate_z.at[i - 1], r1sem.at[i - 1], (dp, lax.rem(c + i, n)))
    ginj_ref[...] = ginj_ref[...] + sum(reached[1:], reached[0])
    for h in range(heads):
        ch = slice(h * 128, (h + 1) * 128)
        entering = jnp.exp(last[h] - cum_col[h]) * nt(inject, inc[h].astype(BF16))
        gi_ref[:, ch] = (acc[:, ch] + entering).astype(BF16)
    total = rate_mine[...]
    for i in range(n - 1):
        arrived(rate_z.at[i], r1sem.at[i])
        total = total + rate_z[i]
    rate_mid[...] = total
    for i in range(1, dps):
        send(rate_mid, rate_dp.at[i - 1], r2sem.at[i - 1], (lax.rem(dp + i, dps), c))

    at = pl.ds(pl.multiple_of(c * rows, rows), rows)
    result = own[0, at, :]
    for i in range(n - 1):
        arrived(zrecv.at[i], dsem.at[i])
        result = result + zrecv[i].astype(F32)
    gw_ref[...] = result

    for i in range(dps - 1):
        arrived(rate_dp.at[i], r2sem.at[i])
        total = total + rate_dp[i]
    whole = jnp.sum(total, axis=1, keepdims=True) / (length * dps * n)
    rate_out[...] = jnp.broadcast_to(whole, rate_out.shape)

    for copy, cond in sent:
        if cond is None:
            copy.wait_send()
        else:
            pl.when(cond)(lambda: copy.wait_send())


def hand_over(*refs):
    for i in range(4):
        refs[4 + i][...] = refs[i][...]


def local(n, dps, cotangent, out_weight, head_input, injector, readout, decay_code, decay_rate, start_state):
    length, width = cotangent.shape[1:]
    channels, dz = out_weight.shape
    heads = decay_rate.shape[0]
    chips = dps // 2
    rows, cols = channels // n, width // dps
    code = decay_code[0]
    parts = jnp.concatenate([code // 256, code % 256], axis=1).astype(BF16)
    code_col = jnp.pad(parts, ((0, 0), (0, 128 - 2 * heads)))
    sends = 2 + 2 * (n - 2) + 6 * (n - 1) + chips + 2 * (chips - 1) + 2 * heads + 2 * (n - 1) + (dps - 1)
    vmem = pl.BlockSpec(memory_space=pltpu.VMEM)
    dma = pltpu.SemaphoreType.DMA
    gi, ginj, gread, gw, rate = pl.pallas_call(
        functools.partial(kernel, n, dps),
        out_shape=(
            jax.ShapeDtypeStruct((length, channels), BF16),
            jax.ShapeDtypeStruct((length, 128), F32),
            jax.ShapeDtypeStruct((length, 128), F32),
            jax.ShapeDtypeStruct((rows, cols), F32),
            jax.ShapeDtypeStruct((8, 128), F32),
        ),
        in_specs=[pl.BlockSpec(memory_space=pltpu.SMEM), pl.BlockSpec(memory_space=pl.ANY)] + [vmem] * 6,
        out_specs=(vmem,) * 5,
        scratch_shapes=[
            pltpu.VMEM((length, width), BF16),
            pltpu.VMEM((2, n - 1, channels, dz), BF16),
            pltpu.VMEM((length, channels), F32),
            pltpu.VMEM((chips, channels, cols), F32),
            pltpu.VMEM((chips, channels, cols), BF16),
            pltpu.VMEM((chips, channels, cols), BF16),
            pltpu.VMEM((2, chips - 1, channels // 2, cols), BF16),
            pltpu.VMEM((2, chips - 1, channels // 2, cols), BF16),
            pltpu.VMEM((n - 1, rows, cols), BF16),
            pltpu.VMEM((n - 1, rows, cols), BF16),
            pltpu.VMEM((channels, length), BF16),
            pltpu.VMEM((heads, length, length), BF16),
            pltpu.VMEM((heads, length, length), F32),
            pltpu.VMEM((heads, length, length), F32),
            pltpu.VMEM((heads, length, length), F32),
            pltpu.VMEM((heads, length, 256), BF16),
            pltpu.VMEM((heads, 128, 128), F32),
            pltpu.VMEM((heads, 128, 128), F32),
            pltpu.VMEM((n - 1, 8, 128), F32),
            pltpu.VMEM((dps - 1, 8, 128), F32),
            pltpu.VMEM((8, 128), F32),
            pltpu.VMEM((8, 128), F32),
            dma((4,)),
            dma((sends,)),
            dma((2, n - 1)),
            dma((2, n - 1)),
            dma((2, n - 1, 2)),
            dma((chips,)),
            dma((2, chips - 1)),
            dma((n - 1,)),
            dma((heads,)),
            dma((n - 1,)),
            dma((dps - 1,)),
        ],
        compiler_params=pltpu.CompilerParams(
            collective_id=0, has_side_effects=True, vmem_limit_bytes=60 * 1024 * 1024
        ),
        cost_estimate=pl.CostEstimate(flops=10**10, bytes_accessed=2 * 10**7, transcendentals=10**6),
    )(
        decay_rate, cotangent[0], out_weight, head_input[0], injector[0], readout[0],
        code_col, start_state[0, 0],
    )
    results = (gi, ginj, gread, gw)
    gi, ginj, gread, gw = pl.pallas_call(
        hand_over,
        out_shape=tuple(jax.ShapeDtypeStruct(part.shape, part.dtype) for part in results),
        in_specs=[vmem] * 4,
        out_specs=(vmem,) * 4,
    )(*results)
    return gi[None], ginj[None], gread[None], gw, rate[:heads, 0]


def solution(mesh):
    n, dps = mesh.shape["ctx"], mesh.shape["dp"]
    in_specs = (
        P("dp", "ctx", None),
        P(None, "ctx"),
        P("dp", "ctx", None),
        P("dp", "ctx", None),
        P("dp", "ctx", None),
        P("dp", "ctx", None),
        P(),
        P("dp", "ctx", None, None, None),
    )
    out_specs = (
        P("dp", "ctx", None),
        P("dp", "ctx", None),
        P("dp", "ctx", None),
        P("ctx", "dp"),
        P(),
    )
    return jax.shard_map(
        functools.partial(local, n, dps), mesh=mesh, in_specs=in_specs, out_specs=out_specs, check_vma=False
    )
```

```python
import functools

import jax
import jax.numpy as jnp
from jax import lax
from jax.experimental import pallas as pl
from jax.experimental.pallas import tpu as pltpu
from jax.sharding import PartitionSpec as P

F32, BF16 = jnp.float32, jnp.bfloat16
MESH = pl.DeviceIdType.MESH


def nn(a, b):
    return lax.dot_general(a, b, (((1,), (0,)), ((), ())), preferred_element_type=F32)


def nt(a, b):
    return lax.dot_general(a, b, (((1,), (1,)), ((), ())), preferred_element_type=F32)


def halves(value):
    high = value.astype(BF16)
    return high, (value - high.astype(F32)).astype(BF16)


def fold(row):
    total = row[:, :128]
    for at in range(128, row.shape[1], 128):
        total = total + row[:, at : at + 128]
    return total


def kernel(
    n, dps,
    rate_ref, cot_hbm, w_ref, x_ref, inj_ref, read_ref, codecol_ref, start_ref,
    gi_ref, ginj_ref, gread_ref, gw_ref, rate_out,
    cot, wslot, acc, own, part_send, part_recv, plane_send, plane_recv, zsend, zrecv,
    fwd_t, mix_t, wts, wts_t, qts, scal, inc, chain_send, rate_z, rate_dp, rate_mine, rate_mid,
    cot_sem, send_sem, zsem, psem, csem, asem, bsem, dsem, chsem, r1sem, r2sem,
):
    length, heads = x_ref.shape[0], start_ref.shape[0]
    dz = w_ref.shape[1]
    chips = dps // 2
    rows, cols = gw_ref.shape
    dp, c = lax.axis_index("dp"), lax.axis_index("ctx")
    chip, core = lax.div(dp, 2), lax.rem(dp, 2)
    partner = (chip * 2 + 1 - core, c)
    quarter = w_ref.shape[0] // 4
    sent = []
    counter = [0]

    def send(src, dst, recv_sem, device, cond=None):
        index = counter[0]
        counter[0] += 1
        copy = pltpu.make_async_remote_copy(
            src_ref=src, dst_ref=dst, send_sem=send_sem.at[index], recv_sem=recv_sem,
            device_id=device, device_id_type=MESH,
        )
        sent.append((copy, cond))
        if cond is None:
            copy.start()
        else:
            pl.when(cond)(lambda: copy.start())

    def arrived(dst, recv_sem):
        pltpu.make_async_copy(dst, dst, recv_sem).wait()

    loads = []
    for i in range(4):
        r = pl.ds(i * (length // 4), length // 4)
        load = pltpu.make_async_copy(cot_hbm.at[r], cot.at[r], cot_sem.at[i])
        load.start()
        loads.append(load)

    barrier = pltpu.get_barrier_semaphore()
    for i in range(1, dps):
        pl.semaphore_signal(barrier, inc=1, device_id=(lax.rem(dp + i, dps), c), device_id_type=MESH)
    for i in range(1, n):
        pl.semaphore_signal(barrier, inc=1, device_id=(dp, lax.rem(c + i, n)), device_id_type=MESH)
    pl.semaphore_wait(barrier, dps + n - 2)

    def shard_place(shard):
        par = lax.rem(shard, 2)
        bit = lax.rem(chip, 2) * (1 - par) + lax.rem(lax.div(chip, 2), 2) * par
        peer = chip + (1 - 2 * bit) * (1 + par)
        return bit, peer

    def q_rows(k, bit):
        return pl.ds(pl.multiple_of((2 * k + bit) * quarter, quarter), quarter)

    bit, _ = shard_place(c)
    mine = q_rows(core, bit)
    send(w_ref.at[mine], wslot.at[0, 0, mine], zsem.at[0, 0], (dp, lax.rem(c + 1, n)), c + 1 < n)
    send(w_ref.at[mine], wslot.at[1, 0, mine], zsem.at[1, 0], (dp, lax.rem(c + n - 1, n)), c > 0)

    def shard_of(way, step):
        return (c - 1 - step, c - 1 - step >= 0) if way == 0 else (c + 1 + step, c + 1 + step < n)

    def w_z(step):
        for way in range(2):
            shard, valid = shard_of(way, step)
            shard = lax.rem(shard + n, n)
            bit, peer = shard_place(shard)
            here = q_rows(core, bit)
            slot = wslot.at[way, step, here]
            pl.when(valid)(lambda: arrived(slot, zsem.at[way, step]))
            if step + 1 < n - 1:
                if way == 0:
                    send(slot, wslot.at[way, step + 1, here], zsem.at[way, step + 1],
                         (dp, lax.rem(c + 1, n)), valid & (c + 1 < n))
                else:
                    send(slot, wslot.at[way, step + 1, here], zsem.at[way, step + 1],
                         (dp, lax.rem(c + n - 1, n)), valid & (c > 0))
            send(slot, slot, psem.at[way, step], (peer * 2 + core, c), valid)
            send(slot, slot, csem.at[way, step, 0], partner, valid)

    def w_plane(step):
        for way in range(2):
            shard, valid = shard_of(way, step)
            shard = lax.rem(shard + n, n)
            bit, _ = shard_place(shard)
            slot = wslot.at[way, step, q_rows(core, 1 - bit)]
            pl.when(valid)(lambda: arrived(slot, psem.at[way, step]))
            send(slot, slot, csem.at[way, step, 1], partner, valid)

    def w_use(step):
        for way in range(2):
            shard, valid = shard_of(way, step)
            shard = lax.rem(shard + n, n)
            bit, _ = shard_place(shard)

            @pl.when(valid)
            def _():
                for which in range(2):
                    there = bit if which == 0 else 1 - bit
                    arrived(wslot.at[way, step, q_rows(1 - core, there)], csem.at[way, step, which])
                at = pl.ds(pl.multiple_of(shard * dz, dz), dz)
                acc[...] += nt(cot[:, at], wslot[way, step])

    row_at = lax.broadcasted_iota(jnp.int32, (length, length), 0)
    col_at = lax.broadcasted_iota(jnp.int32, (length, length), 1)
    lower = row_at >= col_at
    upper = col_at >= row_at
    col_sum = nn(jnp.where(lower, 1.0, 0.0).astype(BF16), codecol_ref[...])
    row_sum = col_sum.T
    inter_t = nt(inj_ref[...], read_ref[...])
    x_t = x_ref[...].astype(F32).T.astype(BF16)
    cum_col, cum_row = [], []
    for h in range(heads):
        ch = slice(h * 128, (h + 1) * 128)
        rate = rate_ref[h]
        cc = -rate * (256.0 * col_sum[:, h : h + 1] + col_sum[:, heads + h : heads + h + 1])
        cr = -rate * (256.0 * row_sum[h : h + 1] + row_sum[heads + h : heads + h + 1])
        cum_col.append(cc)
        cum_row.append(cr)
        w_t = jnp.where(upper, jnp.exp(jnp.where(upper, cr - cc, 0.0)), 0.0)
        wts_t[h] = w_t
        mixed = (inter_t * w_t).astype(BF16)
        mix_t[h] = mixed
        high, low = halves(start_ref[h])
        carried = nt(high, read_ref[...]) + nt(low, read_ref[...])
        fwd_t[ch, :] = (nn(x_t[ch], mixed) + jnp.exp(cr) * carried).astype(BF16)

    for load in loads:
        load.wait()

    def block(chip_at, core_at):
        at = pl.ds(pl.multiple_of((chip_at * 2 + core_at) * cols, cols), cols)
        return nn(fwd_t[...], cot[:, at])

    levels = chips.bit_length() - 1
    bits = [lax.rem(lax.div(chip, 1 << k), 2) for k in range(levels)]

    def chip_across(offset):
        return chip + sum(((1 << k) * (1 - 2 * bits[k]) for k in range(levels) if offset >> k & 1), 0)

    half = fwd_t.shape[0] // 2
    ways = (list(range(levels)), list(range(levels))[::-1])

    def leaving(way, level):
        keys = ways[way]
        return [r for r in range(chips) if r >> keys[level] & 1 and not any(r >> keys[k] & 1 for k in range(level))]

    def plane_out(way, level, r):
        bit_at = 1 << ways[way][level]
        at = slice(way * half, (way + 1) * half)
        plane_send[way, r - 1] = own[r, at].astype(BF16)
        send(plane_send.at[way, r - 1], plane_recv.at[way, r - 1], bsem.at[way, r - 1],
             (chip_across(bit_at) * 2 + core, c))

    def plane_in(level):
        for way in range(2):
            bit_at = 1 << ways[way][level]
            at = slice(way * half, (way + 1) * half)
            for r in leaving(way, level):
                arrived(plane_recv.at[way, r - 1], bsem.at[way, r - 1])
                own[r - bit_at, at] = own[r - bit_at, at] + plane_recv[way, r - 1].astype(F32)
            if level + 1 < levels:
                for r in leaving(way, level + 1):
                    plane_out(way, level + 1, r)

    first = [r for r in range(1, chips) if r & 1 and r >> (levels - 1) & 1]
    order = first + [r for r in range(chips - 1, -1, -1) if r not in first]
    for r in order:
        part_send[r] = block(chip_across(r), 1 - core).astype(BF16)
        send(part_send.at[r], part_recv.at[r], asem.at[r], partner)
    w_z(0)
    for r in order:
        mine_too = block(chip_across(r), core)
        arrived(part_recv.at[r], asem.at[r])
        own[r] = mine_too + part_recv[r].astype(F32)
        for way in range(2):
            if r in leaving(way, 0):
                plane_out(way, 0, r)

    own_product = lambda: nt(cot[:, pl.ds(pl.multiple_of(c * dz, dz), dz)], w_ref[...])
    for step in range(1, n - 1):
        w_z(step)
        w_plane(step - 1)
        if step == 1:
            acc[...] = own_product()
            inter = nt(read_ref[...], inj_ref[...])
            for h in range(heads):
                spread = jnp.where(lower, cum_col[h] - cum_row[h], 0.0)
                weight = jnp.where(lower, jnp.exp(spread), 0.0)
                wts[h] = weight
                qts[h] = inter * weight * spread
                high, low = halves(jnp.exp(cum_col[h]) * read_ref[...].astype(F32))
                scal[h, :, :128] = high
                scal[h, :, 128:] = low
        else:
            w_use(step - 2)
    w_use(n - 3)
    for level in range(levels - 1):
        plane_in(level)
    w_plane(n - 2)
    w_use(n - 2)

    grad = acc[...].astype(BF16)
    grad_t = grad.astype(F32).T.astype(BF16)
    last = [cum_col[h][length - 1 : length, :] for h in range(heads)]
    pieces = []
    for h in range(heads):
        both = nn(grad_t[h * 128 : (h + 1) * 128], scal[h])
        pieces.append(both[:, :128] + both[:, 128:])
    before = (dp, lax.rem(c + n - 1, n))

    @pl.when(c == n - 1)
    def _():
        inc[...] = jnp.zeros_like(inc)

    for h in range(heads):
        chain_send[h] = pieces[h]
        send(chain_send.at[h], inc.at[h], chsem.at[h], before, c == n - 1)

    inject, read = inj_ref[...], read_ref[...]
    pair = pair_t = None
    rates = []
    through_sum = None
    for h in range(heads):
        ch = slice(h * 128, (h + 1) * 128)
        raw = nt(grad[:, ch], x_ref[:, ch])
        raw_t = nt(x_ref[:, ch], grad[:, ch])
        one, one_t = raw * wts[h], raw_t * wts_t[h]
        pair = one if pair is None else pair + one
        pair_t = one_t if pair_t is None else pair_t + one_t
        rate_row = fold(jnp.sum(raw * qts[h], axis=0, keepdims=True))
        high, low = halves(start_ref[h])
        through = jnp.exp(cum_col[h]) * (nn(grad[:, ch], high) + nn(grad[:, ch], low))
        through_sum = through if through_sum is None else through_sum + through
        rate_row = rate_row + jnp.sum(cum_col[h] * (through * read.astype(F32)), axis=0, keepdims=True)
        rates.append(rate_row)
    gread_ref[...] = nn(pair.astype(BF16), inject) + through_sum
    ginj_ref[...] = nn(pair_t.astype(BF16), read)
    for h in range(heads):
        ch = slice(h * 128, (h + 1) * 128)
        acc[:, ch] = nn(mix_t[h], grad[:, ch])
    plane_in(levels - 1)
    for i in range(1, n):
        target = lax.rem(c + i, n)
        at = pl.ds(pl.multiple_of(target * rows, rows), rows)
        zsend[i - 1] = own[0, at, :].astype(BF16)
        send(zsend.at[i - 1], zrecv.at[i - 1], dsem.at[i - 1], (dp, target))

    for h in range(heads):
        @pl.when(c < n - 1)
        def _():
            arrived(inc.at[h], chsem.at[h])

        @pl.when((c < n - 1) & (c > 0))
        def _():
            chain_send[h] = chain_send[h] + jnp.exp(last[h]) * inc[h]

        send(chain_send.at[h], inc.at[h], chsem.at[h], before, (c < n - 1) & (c > 0))

    rate_mine[...] = jnp.zeros_like(rate_mine)
    reached = []
    for h in range(heads):
        ch = slice(h * 128, (h + 1) * 128)
        left = last[h] - cum_col[h]
        high, low = halves(inc[h])
        reach = jnp.exp(left) * (nn(x_ref[:, ch], high) + nn(x_ref[:, ch], low))
        reached.append(reach)
        row = rates[h] + jnp.sum(left * (reach * inject.astype(F32)), axis=0, keepdims=True)
        row = row + (jnp.exp(last[h]) * last[h]) * jnp.sum(inc[h] * start_ref[h], axis=0, keepdims=True)
        rate_mine[h : h + 1, :] = row
    for i in range(1, n):
        send(rate_mine, rate_z.at[i - 1], r1sem.at[i - 1], (dp, lax.rem(c + i, n)))
    ginj_ref[...] = ginj_ref[...] + sum(reached[1:], reached[0])
    for h in range(heads):
        ch = slice(h * 128, (h + 1) * 128)
        entering = jnp.exp(last[h] - cum_col[h]) * nt(inject, inc[h].astype(BF16))
        gi_ref[:, ch] = (acc[:, ch] + entering).astype(BF16)
    total = rate_mine[...]
    for i in range(n - 1):
        arrived(rate_z.at[i], r1sem.at[i])
        total = total + rate_z[i]
    rate_mid[...] = total
    for i in range(1, dps):
        send(rate_mid, rate_dp.at[i - 1], r2sem.at[i - 1], (lax.rem(dp + i, dps), c))

    at = pl.ds(pl.multiple_of(c * rows, rows), rows)
    result = own[0, at, :]
    for i in range(n - 1):
        arrived(zrecv.at[i], dsem.at[i])
        result = result + zrecv[i].astype(F32)
    gw_ref[...] = result

    for i in range(dps - 1):
        arrived(rate_dp.at[i], r2sem.at[i])
        total = total + rate_dp[i]
    whole = jnp.sum(total, axis=1, keepdims=True) / (length * dps * n)
    rate_out[...] = jnp.broadcast_to(whole, rate_out.shape)

    for copy, cond in sent:
        if cond is None:
            copy.wait_send()
        else:
            pl.when(cond)(lambda: copy.wait_send())


def hand_over(*refs):
    for i in range(4):
        refs[5 + i][...] = refs[i][...]
    for h in range(refs[9].shape[0]):
        refs[9][h] = refs[4][h, 0]


def local(n, dps, cotangent, out_weight, head_input, injector, readout, decay_code, decay_rate, start_state):
    length, width = cotangent.shape[1:]
    channels, dz = out_weight.shape
    heads = decay_rate.shape[0]
    chips = dps // 2
    rows, cols = channels // n, width // dps
    code = decay_code[0]
    parts = jnp.concatenate([code // 256, code % 256], axis=1).astype(BF16)
    code_col = jnp.pad(parts, ((0, 0), (0, 128 - 2 * heads)))
    sends = 2 + 2 * (n - 2) + 6 * (n - 1) + chips + 2 * (chips - 1) + 2 * heads + 2 * (n - 1) + (dps - 1)
    vmem = pl.BlockSpec(memory_space=pltpu.VMEM)
    dma = pltpu.SemaphoreType.DMA
    gi, ginj, gread, gw, rate = pl.pallas_call(
        functools.partial(kernel, n, dps),
        out_shape=(
            jax.ShapeDtypeStruct((length, channels), BF16),
            jax.ShapeDtypeStruct((length, 128), F32),
            jax.ShapeDtypeStruct((length, 128), F32),
            jax.ShapeDtypeStruct((rows, cols), F32),
            jax.ShapeDtypeStruct((8, 128), F32),
        ),
        in_specs=[pl.BlockSpec(memory_space=pltpu.SMEM), pl.BlockSpec(memory_space=pl.ANY)] + [vmem] * 6,
        out_specs=(vmem,) * 5,
        scratch_shapes=[
            pltpu.VMEM((length, width), BF16),
            pltpu.VMEM((2, n - 1, channels, dz), BF16),
            pltpu.VMEM((length, channels), F32),
            pltpu.VMEM((chips, channels, cols), F32),
            pltpu.VMEM((chips, channels, cols), BF16),
            pltpu.VMEM((chips, channels, cols), BF16),
            pltpu.VMEM((2, chips - 1, channels // 2, cols), BF16),
            pltpu.VMEM((2, chips - 1, channels // 2, cols), BF16),
            pltpu.VMEM((n - 1, rows, cols), BF16),
            pltpu.VMEM((n - 1, rows, cols), BF16),
            pltpu.VMEM((channels, length), BF16),
            pltpu.VMEM((heads, length, length), BF16),
            pltpu.VMEM((heads, length, length), F32),
            pltpu.VMEM((heads, length, length), F32),
            pltpu.VMEM((heads, length, length), F32),
            pltpu.VMEM((heads, length, 256), BF16),
            pltpu.VMEM((heads, 128, 128), F32),
            pltpu.VMEM((heads, 128, 128), F32),
            pltpu.VMEM((n - 1, 8, 128), F32),
            pltpu.VMEM((dps - 1, 8, 128), F32),
            pltpu.VMEM((8, 128), F32),
            pltpu.VMEM((8, 128), F32),
            dma((4,)),
            dma((sends,)),
            dma((2, n - 1)),
            dma((2, n - 1)),
            dma((2, n - 1, 2)),
            dma((chips,)),
            dma((2, chips - 1)),
            dma((n - 1,)),
            dma((heads,)),
            dma((n - 1,)),
            dma((dps - 1,)),
        ],
        compiler_params=pltpu.CompilerParams(
            collective_id=0, has_side_effects=True, vmem_limit_bytes=60 * 1024 * 1024
        ),
        cost_estimate=pl.CostEstimate(flops=10**10, bytes_accessed=2 * 10**7, transcendentals=10**6),
    )(
        decay_rate, cotangent[0], out_weight, head_input[0], injector[0], readout[0],
        code_col, start_state[0, 0],
    )
    smem = pl.BlockSpec(memory_space=pltpu.SMEM)
    results = (gi, ginj, gread, gw)
    gi, ginj, gread, gw, rate = pl.pallas_call(
        hand_over,
        out_shape=tuple(jax.ShapeDtypeStruct(part.shape, part.dtype) for part in results)
        + (jax.ShapeDtypeStruct((heads,), F32),),
        in_specs=[vmem] * 4 + [smem],
        out_specs=(vmem,) * 4 + (smem,),
    )(*results, rate)
    return gi[None], ginj[None], gread[None], gw, rate


def solution(mesh):
    n, dps = mesh.shape["ctx"], mesh.shape["dp"]
    in_specs = (
        P("dp", "ctx", None),
        P(None, "ctx"),
        P("dp", "ctx", None),
        P("dp", "ctx", None),
        P("dp", "ctx", None),
        P("dp", "ctx", None),
        P(),
        P("dp", "ctx", None, None, None),
    )
    out_specs = (
        P("dp", "ctx", None),
        P("dp", "ctx", None),
        P("dp", "ctx", None),
        P("ctx", "dp"),
        P(),
    )
    return jax.shard_map(
        functools.partial(local, n, dps), mesh=mesh, in_specs=in_specs, out_specs=out_specs, check_vma=False
    )
```
